256 devices in a mesh: wide: 32 (over z_hi, x, y), narrow: 8 (over z_lo, core).
Axes of the slice: x: 4, y: 4, z: 8 (z_hi: 2, z_lo: 4; z = z_hi * 4 + z_lo), core: 2. Of those that a mesh axis runs over, the one named last changes fastest.
Arguments:
- aux_vectors: float32 [4096, 8192], P('narrow', 'wide'), may hold values from -0.6 to 0.6
- occ_index: int32 [4096], P('narrow'), may hold values from 0 to 199
- vir_index: int32 [4096], P('narrow'), may hold values from 0 to 1999
- occ_energy: float32 [200], replicated, may hold values from -1.5 to -0.3
- vir_energy: float32 [2000], replicated, may hold values from 0.1 to 3
- frequency: float32 [1], replicated, may hold values from 0.2 to 2
Outputs:
- polar: float32 [8192, 8192], P('wide', 'narrow')
The draws below stay inside these ranges and needn't reach their ends.
All inputs are finite; a program needn't handle non-finite values.
Results may differ from the reference program's by a relative error of at most 0.000055.
Values sent between devices are 32-bit elements; how exact they have to be, the bound alone decides.
A program may use at most 128 MiB of HBM per device.

```python
import math
import jax
import jax.numpy as jnp
from jax import lax

NOCC = 200
NVIR = 2000
NAUX = 8192
NIA = 4096


def touch_ends(drawn, own_key, smallest, largest):
    longest = drawn.shape.index(max(drawn.shape))
    spots = []
    for shift in (0, 1):
        where = [jax.random.randint(jax.random.fold_in(own_key, axis), (), 0, length) for axis, length in enumerate(drawn.shape)]
        where[longest] = (where[longest] + shift) % drawn.shape[longest]
        spots.append(tuple(where))
    return drawn.at[spots[0]].set(smallest).at[spots[1]].set(largest)


def block_scale(stream_key, shape, pieces, smallest, high):
    def one(axis_at, parts):
        heights = jax.random.uniform(jax.random.fold_in(jax.random.fold_in(stream_key, 6), axis_at), (parts,), jnp.float32, smallest / len(pieces), high / len(pieces))
        return jnp.repeat(jnp.exp(heights), shape[axis_at] // parts).reshape((-1,) + (1,) * (len(shape) - axis_at - 1))

    gain = one(*pieces[0])
    for cut in pieces[1:]:
        gain = gain * one(*cut)
    return gain


def bell_draw(key, dims, scale, limit, split=(), held_as=jnp.bfloat16):
    result = scale * jax.random.normal(key, dims, jnp.float32)
    if split:
        result = result * block_scale(key, dims, split, -0.22, 0.18)
    return jnp.clip(result, -limit, limit).astype(held_as)


def setup_inputs(seed: int = 0) -> dict:
    key_of = jax.random.split(jax.random.key(seed), 7)
    aux_vectors = bell_draw(key_of[0], (NIA, NAUX), 0.1, 0.6, ((0, 8), (1, 32)), jnp.float32)
    occ_index = touch_ends(jax.random.randint(key_of[1], (NIA,), 0, NOCC), jax.random.fold_in(key_of[1], 1), 0, NOCC - 1).astype(jnp.int32)
    vir_index = touch_ends(jax.random.randint(key_of[2], (NIA,), 0, NVIR), jax.random.fold_in(key_of[2], 1), 0, NVIR - 1).astype(jnp.int32)
    occ_energy = jnp.clip(jax.random.uniform(key_of[3], (NOCC,), jnp.float32, -1.5, -0.3), -1.5, -0.3)
    vir_energy = jnp.clip(jax.random.uniform(key_of[4], (NVIR,), jnp.float32, 0.1, 3.0), 0.1, 3.0)
    frequency = jnp.clip(jnp.exp(jax.random.uniform(key_of[5], (1,), jnp.float32, math.log(0.2), math.log(2.0))), 0.2, 2.0)
    return {"aux_vectors": aux_vectors, "occ_index": occ_index, "vir_index": vir_index, "occ_energy": occ_energy, "vir_energy": vir_energy, "frequency": frequency}


def reference(aux_vectors, occ_index, vir_index, occ_energy, vir_energy, frequency):
    gap = vir_energy[vir_index] - occ_energy[occ_index]
    omega = frequency[0]
    weights = 2.0 * gap / (gap * gap + omega * omega)
    scaled = aux_vectors * weights[:, None]
    return jnp.dot(scaled.T, aux_vectors, precision=lax.Precision.HIGHEST, preferred_element_type=jnp.float32)
```

```python
import jax
import jax.numpy as jnp
from jax import lax
from jax.experimental import pallas as pl
from jax.experimental.pallas import tpu as pltpu
from jax.sharding import PartitionSpec as P

MESH = pl.DeviceIdType.MESH
F32, BF16 = jnp.float32, jnp.bfloat16


def lookup(indices, table):
    columns = jnp.arange(table.shape[0], dtype=jnp.int32)
    return jnp.sum(jnp.where(indices[:, None] == columns[None, :], table[None, :], 0.0), axis=1)


def kernel(a_ref, w_ref, out_ref, G, J, W, RH, RL, acc, other, land,
           zs, zr, ws, wr, s1s, s1r, s2s, s2r, s3s, s3r, ds, dr, as_, ar):
    wide, narrow = lax.axis_index("wide"), lax.axis_index("narrow")
    zh, x, y = wide // 16, (wide // 4) % 4, wide % 4
    zl, c = narrow // 2, narrow % 2
    pos = zh * 4 + zl
    h, pi = zl % 2, zl // 2
    is_src = (x + y) % 2 == pi
    i_own, j_own = x // 2, y // 2

    def at(x_=x, y_=y, pos_=pos, c_=c):
        return ((pos_ // 4) * 16 + x_ * 4 + y_, (pos_ % 4) * 2 + c_)

    def remote(src, dst, send, recv, device):
        return pltpu.make_async_remote_copy(
            src_ref=src, dst_ref=dst, send_sem=send, recv_sem=recv, device_id=device, device_id_type=MESH)

    xs = [(x + d) % 4 for d in range(4)]
    ys = [(y + d) % 4 for d in range(4)]

    barrier = pltpu.get_barrier_semaphore()
    friends = [at(x_=xs[d]) for d in (1, 2, 3)] + [at(y_=ys[d]) for d in (1, 2, 3)]
    friends += [at(pos_=(pos + d) % 8) for d in range(1, 8)] + [at(c_=1 - c)]
    for device in friends:
        pl.semaphore_signal(barrier, inc=1, device_id=device, device_id_type=MESH)
    G[pos, 0] = a_ref[0:256, :]
    G[pos, 1] = a_ref[256:512, :]
    W[zl] = w_ref[...]
    pl.semaphore_wait(barrier, len(friends))

    def z_copy(way, d, half):
        q = (pos + 8 + (-d if way == 0 else d)) % 8
        to = (pos + (1 if way == 0 else 7)) % 8
        block = G.at[q, half]
        return remote(block, block, zs.at[way, d, half], zr.at[way, d, half], at(pos_=to))

    def z_wait(way, d, half):
        q = (pos + 8 + (-d if way == 0 else d)) % 8
        block = G.at[q, half]
        remote(block, block, zs.at[way, d - 1, half], zr.at[way, d - 1, half], at(pos_=(pos + 1) % 8)).wait_recv()

    def w_copy(t):
        return remote(W.at[zl], W.at[zl], ws.at[t], wr.at[zl], at(pos_=zh * 4 + (zl + t) % 4))

    def first(zq, half, t):
        d = (1, 3, 2)[t]
        piece = J.at[zq, y, i_own, half]
        if half == 0:
            return remote(piece, piece, s1s.at[zq, half, t], s1r.at[zq, half, i_own], at(x_=xs[d]))
        return remote(piece, piece, s1s.at[zq, half, t], s1r.at[zq, half, j_own], at(y_=ys[d]))

    def piece_of(zq, half, shift, k):
        if half == 0:
            return J.at[zq, ys[shift], k, half]
        return J.at[zq, 2 * k + (pi + xs[shift]) % 2, xs[shift] // 2, half]

    def neighbour(half, shift):
        return at(y_=ys[shift]) if half == 0 else at(x_=xs[shift])

    def second(zq, half, way, k):
        piece = piece_of(zq, half, 0, k)
        return remote(piece, piece, s2s.at[zq, half, way, k], s2r.at[zq, half, way, k],
                      neighbour(half, 1 if way == 0 else 3))

    def second_wait(zq, half, way, k):
        piece = piece_of(zq, half, 3 if way == 0 else 1, k)
        remote(piece, piece, s2s.at[zq, half, way, k], s2r.at[zq, half, way, k], neighbour(half, 1)).wait_recv()

    def third(zq, half, way):
        piece = piece_of(zq, half, 3 if way == 0 else 1, way)
        return remote(piece, piece, s3s.at[zq, half, way], s3r.at[zq, half, way],
                      neighbour(half, 1 if way == 0 else 3))

    def third_wait(zq, half, way):
        piece = piece_of(zq, half, 2, way)
        remote(piece, piece, s3s.at[zq, half, way], s3r.at[zq, half, way], neighbour(half, 1)).wait_recv()

    def stage1(zq, half):
        @pl.when(is_src)
        def _():
            block = G[zh * 4 + zq, half]
            J[zq, y, i_own, half] = jnp.where(h == 0, block[:, :128], block[:, 128:])
            for t in range(3):
                first(zq, half, t).start()

    def stage2(zq, half):
        own = i_own if half == 0 else j_own
        for k in range(2):
            @pl.when(jnp.logical_not(jnp.logical_and(is_src, own == k)))
            def _(k=k):
                piece = piece_of(zq, half, 0, k)
                remote(piece, piece, s1s.at[zq, half, 0], s1r.at[zq, half, k], neighbour(half, 1)).wait_recv()

            for way in range(2):
                second(zq, half, way, k).start()

    def stage3(zq, half):
        for way in range(2):
            second_wait(zq, half, way, way)
            third(zq, half, way).start()

    def stage4(zq, half):
        for way in range(2):
            second_wait(zq, half, way, 1 - way)
            third_wait(zq, half, way)

    def prepare(q, half):
        zq, zhq = q % 4, q // 4
        t = G[q, half].T * W[zq, 0:1, half * 256:half * 256 + 256]
        hi = t.astype(BF16)
        RH[zq, zhq, :, half * 256:half * 256 + 256] = hi
        RL[zq, zhq, :, half * 256:half * 256 + 256] = (t - hi.astype(F32)).astype(BF16)

    def unit(zq, zh1, order=lambda s: s, after=None):
        def body(s, carry):
            y2 = order(s)
            rows = [jnp.concatenate([J[zq, y2, 0, half], J[zq, y2, 1, half]], axis=1) for half in range(2)]
            b = jnp.concatenate(rows, axis=0)
            bh = b.astype(BF16)
            bl = (b - bh.astype(F32)).astype(BF16)
            ah, al = RH[zq, zh1], RL[zq, zh1]
            acc[y2, zh1] += (jnp.dot(ah, bh, preferred_element_type=F32)
                             + jnp.dot(ah, bl, preferred_element_type=F32)
                             + jnp.dot(al, bh, preferred_element_type=F32))
            return carry
        lax.fori_loop(0, 4, body, 0)

    for half in range(2):
        for way in range(2):
            z_copy(way, 0, half).start()
    for t in range(1, 4):
        w_copy(t).start()
    for half in range(2):
        stage1(zl, half)
    acc[...] = jnp.zeros_like(acc)
    for half in range(2):
        prepare(pos, half)
    for half in range(2):
        stage2(zl, half)
    for t in range(1, 4):
        zq = (zl + t) % 4
        remote(W.at[zq], W.at[zq], ws.at[t], wr.at[zq], at(pos_=zh * 4 + zq)).wait_recv()

    def own(d, do):
        if d == 0:
            do(zl)
            return
        for way in range(2):
            zq = zl - d if way == 0 else zl + d
            @pl.when(zq >= 0 if way == 0 else zq <= 3)
            def _(zq=zq):
                do(zq)

    for d in range(1, 5):
        for half in range(2):
            for way in range(2):
                if d == 4 and way != half:
                    continue
                z_wait(way, d, half)
                if d < 3 or (d == 3 and way == half):
                    z_copy(way, d, half).start()
                if d < 4:
                    zq = zl - d if way == 0 else zl + d
                    @pl.when(zq >= 0 if way == 0 else zq <= 3)
                    def _(zq=zq, half=half):
                        stage1(zq, half)
        own(d - 1, lambda zq: [stage3(zq, half) for half in range(2)])
        for half in range(2):
            if d < 4:
                prepare((pos + 8 - d) % 8, half)
                prepare((pos + d) % 8, half)
            else:
                prepare((pos + 4) % 8, half)
        if d < 4:
            own(d, lambda zq: [stage2(zq, half) for half in range(2)])
            own(d - 1, lambda zq: [stage4(zq, half) for half in range(2)])
            own(d - 1, lambda zq: unit(zq, zh))

    def far(zq):
        return jnp.logical_or(zq - zl == 3, zl - zq == 3)

    def rest(zq, carry):
        @pl.when(jnp.logical_not(far(zq)))
        def _():
            unit(zq, 1 - zh)
        return carry

    lax.fori_loop(0, 4, rest, 0)
    yc, yo = (pi + c) % 2, (pi + 1 - c) % 2

    def last(zq):
        for half in range(2):
            stage4(zq, half)
        for zh1 in range(2):
            unit(zq, zh1)

    own(3, last)

    def d_copy(k):
        return remote(acc.at[2 * k + yo], other.at[k], ds.at[k], dr.at[k], at(c_=1 - c))

    for k in range(2):
        d_copy(k).start()

    def a_copy(k, zh1, i):
        y2 = 2 * k + yc
        return remote(acc.at[y2, zh1, :, pl.ds(i * 128, 128)], land.at[y2, h],
                      as_.at[k, zh1, i], ar.at[zl, k], at(pos_=zh1 * 4 + 2 * zh + i))

    def each_out(do, do_self):
        for k in range(2):
            yield_k = k
            for zh1 in range(2):
                for i in range(2):
                    mine = zh1 * 4 + 2 * zh + i == pos

                    @pl.when(jnp.logical_not(mine))
                    def _(zh1=zh1, i=i, k=k):
                        do(k, zh1, i)

                    if do_self is not None:
                        @pl.when(mine)
                        def _(zh1=zh1, i=i, k=k):
                            do_self(k, zh1, i)

    for k in range(2):
        d_copy(k).wait_recv()
        acc[2 * k + yc] += other[k]

    def keep(k, zh1, i):
        land[2 * k + yc, h] = acc[2 * k + yc, zh1, :, i * 128:i * 128 + 128]

    each_out(lambda k, zh1, i: a_copy(k, zh1, i).start(), keep)

    for k in range(2):
        for zs_ in range(4):
            @pl.when((zl // 2) * 4 + zs_ != pos)
            def _(zs_=zs_, k=k):
                y2 = 2 * k + (zs_ // 2 + c) % 2
                block = land.at[y2, zs_ % 2]
                remote(block, block, as_.at[0, 0, 0], ar.at[zs_, k], at(c_=1 - c)).wait_recv()
    for y2 in range(4):
        for hh in range(2):
            out_ref[:, y2 * 256 + hh * 128:y2 * 256 + hh * 128 + 128] = land[y2, hh]

    for way in range(2):
        for half in range(2):
            for d in range(4):
                if d < 3 or way == half:
                    z_copy(way, d, half).wait_send()
    for t in range(1, 4):
        w_copy(t).wait_send()

    def sent(zq, carry):
        for half in range(2):
            @pl.when(is_src)
            def _(half=half):
                for t in range(3):
                    first(zq, half, t).wait_send()
            for way in range(2):
                for k in range(2):
                    second(zq, half, way, k).wait_send()
                third(zq, half, way).wait_send()
        return carry

    lax.fori_loop(0, 4, sent, 0)
    for k in range(2):
        d_copy(k).wait_send()
    each_out(lambda k, zh1, i: a_copy(k, zh1, i).wait_send(), None)


def shards(aux_vectors, occ_index, vir_index, occ_energy, vir_energy, frequency):
    gap = lookup(vir_index, vir_energy) - lookup(occ_index, occ_energy)
    omega = frequency[0]
    weights = 2.0 * gap / (gap * gap + omega * omega)
    weights = jnp.broadcast_to(weights[None, :], (8, 512))
    dma = pltpu.SemaphoreType.DMA
    return pl.pallas_call(
        kernel,
        out_shape=jax.ShapeDtypeStruct((256, 1024), F32),
        in_specs=[pl.BlockSpec(memory_space=pltpu.VMEM)] * 2,
        out_specs=pl.BlockSpec(memory_space=pltpu.VMEM),
        scratch_shapes=[
            pltpu.VMEM((8, 2, 256, 256), F32),
            pltpu.VMEM((4, 4, 2, 2, 256, 128), F32),
            pltpu.VMEM((4, 8, 512), F32),
            pltpu.VMEM((4, 2, 256, 512), BF16),
            pltpu.VMEM((4, 2, 256, 512), BF16),
            pltpu.VMEM((4, 2, 256, 256), F32),
            pltpu.VMEM((2, 2, 256, 256), F32),
            pltpu.VMEM((4, 2, 256, 128), F32),
            dma((2, 4, 2)), dma((2, 4, 2)),
            dma((4,)), dma((4,)),
            dma((4, 2, 3)), dma((4, 2, 2)),
            dma((4, 2, 2, 2)), dma((4, 2, 2, 2)),
            dma((4, 2, 2)), dma((4, 2, 2)),
            dma((2,)), dma((2,)),
            dma((2, 2, 2)), dma((4, 2)),
        ],
        compiler_params=pltpu.CompilerParams(
            collective_id=0, has_side_effects=True, vmem_limit_bytes=48 * 2**20),
        cost_estimate=pl.CostEstimate(flops=2 * 3 * 512 * 1024 * 2048, bytes_accessed=2 * 2**20, transcendentals=0),
        name="gather_multiply",
    )(aux_vectors, weights)


def solution(mesh):
    return jax.shard_map(
        shards,
        mesh=mesh,
        in_specs=(P("narrow", "wide"), P("narrow"), P("narrow"), P(), P(), P()),
        out_specs=P("wide", "narrow"),
        check_vma=False,
    )
```

```python
import jax
import jax.numpy as jnp
from jax import lax
from jax.experimental import pallas as pl
from jax.experimental.pallas import tpu as pltpu
from jax.sharding import PartitionSpec as P

MESH = pl.DeviceIdType.MESH
F32, BF16 = jnp.float32, jnp.bfloat16


def lookup(indices, table_ref, quarter, found):
    size = table_ref.shape[0] // 4

    def body(j, found):
        for k in range(10):
            at = quarter * size + j * 10 + k
            found = jnp.where(indices == at, table_ref[at], found)
        return found
    return lax.fori_loop(0, size // 10, body, found)


def kernel(a_ref, occ_index, vir_index, occ_table, vir_table, omega_ref, out_ref, G, J, W, R, acc, other, land,
           zs, zr, ws, wr, s1s, s1r, s2s, s2r, s3s, s3r, ds, dr, as_, ar, ls, os, levels, relay, br, bs,
           occ_ref, vir_ref, occ_energy, vir_energy, frequency, ts):
    wide, narrow = lax.axis_index("wide"), lax.axis_index("narrow")
    zh, x, y = wide // 16, (wide // 4) % 4, wide % 4
    zl, c = narrow // 2, narrow % 2
    pos = zh * 4 + zl
    h, pi = zl // 2, zl % 2

    def at(x_=x, y_=y, pos_=pos, c_=c):
        return ((pos_ // 4) * 16 + x_ * 4 + y_, (pos_ % 4) * 2 + c_)

    def remote(src, dst, send, recv, device):
        return pltpu.make_async_remote_copy(
            src_ref=src, dst_ref=dst, send_sem=send, recv_sem=recv, device_id=device, device_id_type=MESH)

    xs = [(x + d) % 4 for d in range(4)]
    ys = [(y + d) % 4 for d in range(4)]
    step = jnp.where(zl < 2, 1, 3)
    turn = [(zl + t * step) % 4 for t in range(4)]

    barrier = pltpu.get_barrier_semaphore()
    friends = [at(x_=xs[d]) for d in (1, 2, 3)] + [at(y_=ys[d]) for d in (1, 2, 3)]
    friends += [at(pos_=(pos + d) % 8) for d in range(1, 8)] + [at(c_=1 - c)]
    for device in friends:
        pl.semaphore_signal(barrier, inc=1, device_id=device, device_id_type=MESH)

    def load(hh, r):
        return pltpu.make_async_copy(
            a_ref.at[pl.ds(r * 256, 256), pl.ds(hh * 128, 128)], G.at[pos, hh, r], ls.at[hh, r])

    for hh in range(2):
        for r in range(2):
            load(hh, r).start()
    tables = [pltpu.make_async_copy(src, dst, ts.at[n]) for n, (src, dst) in enumerate((
        (occ_index, occ_ref), (vir_index, vir_ref), (occ_table, occ_energy), (vir_table, vir_energy),
        (omega_ref, frequency)))]
    for table in tables:
        table.start()
    pl.semaphore_wait(barrier, len(friends))
    for hh in range(2):
        for r in range(2):
            load(hh, r).wait()

    CHUNKS = [(d, o, r) for o in range(2) for d in (1, 2, 3) for r in range(2)] + [(4, 0, 0), (4, 0, 1)]

    def z_block(way, d, o, r):
        return G.at[(pos + 8 + (-d if way == 0 else d)) % 8, o if way == 1 else 1 - o, r]

    def z_copy(way, d, o, r):
        block = z_block(way, d, o, r)
        return remote(block, block, zs.at[way, d, o, r], zr.at[way, d, o, r],
                      at(pos_=(pos + (1 if way == 0 else 7)) % 8))

    def z_wait(way, d, o, r):
        block = z_block(way, d, o, r)
        remote(block, block, zs.at[way, d - 1, o, r], zr.at[way, d - 1, o, r], at(pos_=(pos + 1) % 8)).wait_recv()

    def z_sent(d, o):
        return d < 3 or o == 0

    def w_copy(t):
        return remote(W.at[zl], W.at[zl], ws.at[t], wr.at[zl], at(pos_=zh * 4 + (zl + t) % 4))

    def line(r, shift):
        return at(x_=xs[shift]) if r == 0 else at(y_=ys[shift])

    def cross(r, shift):
        return at(y_=ys[shift]) if r == 0 else at(x_=xs[shift])

    def behind(s, r):
        return (x - y - pi - 2 * s + 16) % 4 if r == 0 else (y - x + pi + 2 * s) % 4

    def piece(t, s, r, shift):
        y2 = ys[shift] if r == 0 else (xs[shift] - pi - 2 * s + 8) % 4
        return J.at[turn[t], s, y2, r]

    def first(t, s, r, way):
        p = piece(t, s, r, 0)
        return remote(p, p, s1s.at[t, s, r, way], s1r.at[t, s, r], line(r, 1 if way == 0 else 3))

    def second(t, s, r, way):
        p = piece(t, s, r, 0)
        return remote(p, p, s2s.at[t, s, r, way], s2r.at[t, s, r, way], cross(r, 1 if way == 0 else 3))

    def second_wait(t, s, r, way):
        p = piece(t, s, r, 3 if way == 0 else 1)
        remote(p, p, s2s.at[t, s, r, way], s2r.at[t, s, r, way], cross(r, 1)).wait_recv()

    def third(t, s, r):
        way = (t + r) % 2
        p = piece(t, s, r, 3 if way == 0 else 1)
        return remote(p, p, s3s.at[t, s, r], s3r.at[t, s, r], cross(r, 1 if way == 0 else 3))

    def third_wait(t, s, r):
        p = piece(t, s, r, 2)
        remote(p, p, s3s.at[t, s, r], s3r.at[t, s, r], cross(r, 1)).wait_recv()

    def stage1(t, s, r):
        @pl.when(behind(s, r) == 0)
        def _():
            J[turn[t], s, y, r] = G[zh * 4 + turn[t], h, r]
            for way in range(2):
                first(t, s, r, way).start()

    def stage2(t, s, r):
        @pl.when(behind(s, r) != 0)
        def _():
            p = piece(t, s, r, 0)
            remote(p, p, s1s.at[t, s, r, 0], s1r.at[t, s, r], line(r, 1)).wait_recv()

        way = (t + r) % 2

        @pl.when(behind(s, r) == (1 if way == 0 else 3))
        def _():
            first(t, s, r, way).start()

        for w in range(2):
            second(t, s, r, w).start()

    def stage3(t, s, r):
        second_wait(t, s, r, (t + r) % 2)
        third(t, s, r).start()

    def stage4(t, s, r):
        second_wait(t, s, r, 1 - (t + r) % 2)
        third_wait(t, s, r)

    def prepare(q, hh, r):
        zq, zhq = q % 4, q // 4
        w = jnp.concatenate([W[zq, 2 * r:2 * r + 1], W[zq, 2 * r + 1:2 * r + 2]], axis=1)
        v = G[q, hh, r].T * w
        hi = v.astype(BF16)
        rows = pl.ds(pl.multiple_of(hh * 128, 128), 128)
        R[zq, zhq, 0, rows, r * 256:r * 256 + 256] = hi
        R[zq, zhq, 1, rows, r * 256:r * 256 + 256] = (v - hi.astype(F32)).astype(BF16)

    def unit(t, s, zh1):
        zq = turn[t]

        def body(p, carry):
            rows = [jnp.concatenate([J[zq, s, p, r], J[zq, s, p + 2, r]], axis=1) for r in range(2)]
            b = jnp.concatenate(rows, axis=0)
            bh = b.astype(BF16)
            bl = (b - bh.astype(F32)).astype(BF16)
            both = jnp.dot(R[zq, zh1].reshape(512, 512), bh, preferred_element_type=F32)
            acc[s, p, zh1] += both[:256] + both[256:] + jnp.dot(R[zq, zh1, 0], bl, preferred_element_type=F32)
            return carry
        lax.fori_loop(0, 2, body, 0)

    yc = (pi + c) % 2

    def rows_of(e):
        return 1 - zh if e == 0 else zh

    def d_copy(s, e):
        zh1 = rows_of(e)
        return remote(acc.at[s, 1 - yc, zh1], other.at[s, zh1], ds.at[s, e], dr.at[s, e], at(c_=1 - c))

    def goes_to(s, k, e):
        i = ((2 * k + yc + pi + 2 * s) % 4) // 2
        return rows_of(e) * 4 + 2 * zh + i

    def detour(q):
        return jnp.logical_or(jnp.logical_and(pos == 0, q == 4), jnp.logical_and(pos == 7, q == 3))

    def result(s, k, e):
        return acc.at[s, yc, rows_of(e), :, pl.ds(k * 128, 128)]

    def a_copy(s, k, e):
        return remote(result(s, k, e), land.at[2 * k + yc, h],
                      as_.at[s, k, e], ar.at[zl, k], at(pos_=goes_to(s, k, e)))

    def b_copy(s, k):
        return remote(result(s, k, 0), relay.at[s], as_.at[s, k, 0], br.at[s],
                      at(pos_=jnp.where(pos == 0, 6, 1)))

    def c_copy(s):
        zq, i = jnp.where(pos == 6, 0, 3), jnp.where(pos == 6, 0, 1)
        ycq = (zq % 2 + c) % 2
        k = (i + 2 - ((ycq + zq % 2 + 2 * s) % 4) // 2) % 2
        return remote(relay.at[s], land.at[2 * k + ycq, zq // 2], bs.at[s], ar.at[zq, k],
                      at(pos_=jnp.where(pos == 6, 4, 3)))

    passes = jnp.logical_or(pos == 6, pos == 1)

    def send_out(s, e):
        for k in range(2):
            q = goes_to(s, k, e)

            @pl.when(jnp.logical_and(q != pos, jnp.logical_not(detour(q))))
            def _(k=k):
                a_copy(s, k, e).start()

            if e == 0:
                @pl.when(detour(q))
                def _(k=k):
                    b_copy(s, k).start()
            else:
                @pl.when(q == pos)
                def _(k=k):
                    land[2 * k + yc, h] = acc[s, yc, zh, :, k * 128:k * 128 + 128]

    def pass_on(s):
        @pl.when(passes)
        def _():
            remote(relay.at[s], relay.at[s], bs.at[s], br.at[s], at(c_=1 - c)).wait_recv()
            c_copy(s).start()

    def arrive(n, way):
        d, o, r = CHUNKS[n]
        z_wait(way, d, o, r)
        if d < 3:
            z_copy(way, d, o, r).start()

    def launch(d, o):
        for way in range(2):
            for r in range(2):
                z_copy(way, d, o, r).start()

    def ready(n):
        d, o, r = CHUNKS[n]
        for way in range(2):
            prepare((pos + 8 + (-d if way == 0 else d)) % 8, o if way == 1 else 1 - o, r)

    launch(0, 0)

    def weigh(quarter):
        if quarter == 0:
            levels[...] = jnp.zeros_like(levels)
            for table in tables:
                table.wait()
        levels[0] = lookup(vir_ref[...], vir_energy, quarter, levels[0])
        levels[1] = lookup(occ_ref[...], occ_energy, quarter, levels[1])
        if quarter < 3:
            return
        gap = levels[0] - levels[1]
        omega = frequency[0]
        weights = 2.0 * gap / (gap * gap + omega * omega)
        W[zl] = jnp.concatenate([weights, weights], axis=0)
        for t in range(1, 4):
            w_copy(t).start()

    def begin():
        acc[...] = jnp.zeros_like(acc)
        for t in range(1, 4):
            zq = (zl + t) % 4
            remote(W.at[zq], W.at[zq], ws.at[t], wr.at[zq], at(pos_=zh * 4 + zq)).wait_recv()
        for hh in range(2):
            for r in range(2):
                prepare(pos, hh, r)

    def own(t, s):
        unit(t, s, zh)

    def far(t, s):
        unit(t, s, 1 - zh)

    PLAN = (
        "1001 1011 1000 z00",
        "z01 1100 2011 1010",
        "1110 z11 z10 1101",
        "w0 2100 z21 z20",
        "1111 1210 2001 1200",
        "z31 z30 1211 y",
        "1201 2101 w1 w2",
        "w3 2000 z40 z41",
        "c p2 2200 z50",
        "3001 z51 z61 p1",
        "z60 1310 1300 2201",
        "z71 z70 1301 1311",
        "3000 2211 4001 2300",
        "z81 3100 z80 2301",
        "z91 z90 p9 2310",
        "3101 x 3201 2311",
        "p8 za1 3200 3300",
        "2210 3301 p3 p5",
        "za0 p4 4000 2110",
        "p6 u00 p0 zb1",
        "zc1 4101 4100 p7",
        "u10 zb0 zc0 pb",
        "pa v10 pc 4201",
        "zd1 4200 v20 zd0",
        "pd v00 2010 4300",
        "3310 4301 v30 u30",
        "d00 u20 d01 3011",
        "3311 3211 2111 3210",
        "o00 o01 3010 3110",
        "4310 4311 v31 4211",
        "3111 4210 v21 u21",
        "4011 u31 4010 u01",
        "v01 4110 4111 u11",
        "r0 v11 d10 d11",
        "o10 o11 r1",
    )
    for token in [word for words in PLAN for word in words.split()]:
        kind, args = token[0], [int(v, 16) for v in token[1:]]
        if kind == "z":
            arrive(*args)
        elif kind == "y":
            launch(0, 1)
        elif kind == "x":
            launch(3, 0)
        elif kind == "w":
            weigh(*args)
        elif kind == "c":
            begin()
        elif kind == "p":
            ready(args[0])
        elif kind in "1234":
            {"1": stage1, "2": stage2, "3": stage3, "4": stage4}[kind](*args)
        elif kind == "u":
            own(*args)
        elif kind == "v":
            far(*args)
        elif kind == "d":
            d_copy(*args).start()
        elif kind == "o":
            s, e = args
            d_copy(s, e).wait_recv()
            acc[s, yc, rows_of(e)] += other[s, rows_of(e)]
            send_out(s, e)
        elif kind == "r":
            pass_on(*args)

    def put(zq, k):
        y2, hh = 2 * k + (zq % 2 + c) % 2, zq // 2
        columns = pl.ds(pl.multiple_of(y2 * 256 + hh * 128, 128), 128)
        return pltpu.make_async_copy(land.at[y2, hh], out_ref.at[:, columns], os.at[zq, k])

    def part(zq, s):
        return (((2 * (zl % 2) + c - (zq % 2 + c) % 2 - zq % 2 + 4) % 4) // 2 + s) % 2

    for s in range(2):
        for zq in range(4):
            k = part(zq, s)

            @pl.when((zl // 2) * 4 + zq != pos)
            def _(zq=zq, k=k):
                block = land.at[2 * k + (zq % 2 + c) % 2, zq // 2]
                remote(block, block, as_.at[0, 0, 0], ar.at[zq, k], at(c_=1 - c)).wait_recv()

            put(zq, k).start()
    for zq in range(4):
        for k in range(2):
            put(zq, k).wait()

    for way in range(2):
        for d in range(4):
            for o in range(2):
                for r in range(2):
                    if z_sent(d, o):
                        z_copy(way, d, o, r).wait_send()
    for t in range(1, 4):
        w_copy(t).wait_send()
    for s in range(2):
        for t in range(4):
            for r in range(2):
                fwd = (t + r) % 2
                for way in range(2):
                    sends = behind(s, r) == 0
                    if way == fwd:
                        sends = jnp.logical_or(sends, behind(s, r) == (1 if way == 0 else 3))

                    @pl.when(sends)
                    def _(t=t, s=s, r=r, way=way):
                        first(t, s, r, way).wait_send()

                    second(t, s, r, way).wait_send()
                third(t, s, r).wait_send()
        for e in range(2):
            d_copy(s, e).wait_send()
            for k in range(2):
                @pl.when(goes_to(s, k, e) != pos)
                def _(s=s, k=k, e=e):
                    a_copy(s, k, e).wait_send()

        @pl.when(passes)
        def _(s=s):
            c_copy(s).wait_send()


def shards(aux_vectors, occ_index, vir_index, occ_energy, vir_energy, frequency):
    dma = pltpu.SemaphoreType.DMA
    hbm = pl.BlockSpec(memory_space=pltpu.HBM)
    return pl.pallas_call(
        kernel,
        out_shape=jax.ShapeDtypeStruct((256, 1024), F32),
        in_specs=[hbm] * 6,
        out_specs=hbm,
        scratch_shapes=[
            pltpu.VMEM((8, 2, 2, 256, 128), F32),
            pltpu.VMEM((4, 2, 4, 2, 256, 128), F32),
            pltpu.VMEM((4, 8, 128), F32),
            pltpu.VMEM((4, 2, 2, 256, 512), BF16),
            pltpu.VMEM((2, 2, 2, 256, 256), F32),
            pltpu.VMEM((2, 2, 256, 256), F32),
            pltpu.VMEM((4, 2, 256, 128), F32),
            dma((2, 4, 2, 2)), dma((2, 4, 2, 2)),
            dma((4,)), dma((4,)),
            dma((4, 2, 2, 2)), dma((4, 2, 2)),
            dma((4, 2, 2, 2)), dma((4, 2, 2, 2)),
            dma((4, 2, 2)), dma((4, 2, 2)),
            dma((2, 2)), dma((2, 2)),
            dma((2, 2, 2)), dma((4, 2)),
            dma((2, 2)), dma((4, 2)),
            pltpu.VMEM((2, 4, 128), F32),
            pltpu.VMEM((2, 256, 128), F32), dma((2,)), dma((2,)),
            pltpu.VMEM((4, 128), jnp.int32), pltpu.VMEM((4, 128), jnp.int32),
            pltpu.SMEM((200,), F32), pltpu.SMEM((2000,), F32), pltpu.SMEM((1,), F32), dma((5,)),
        ],
        compiler_params=pltpu.CompilerParams(
            collective_id=0, has_side_effects=True, vmem_limit_bytes=63 * 2**20),
        cost_estimate=pl.CostEstimate(flops=2 * 3 * 512 * 1024 * 2048, bytes_accessed=2 * 2**20, transcendentals=0),
        name="gather_multiply",
    )(aux_vectors, occ_index.reshape(4, 128), vir_index.reshape(4, 128), occ_energy, vir_energy, frequency)


def solution(mesh):
    return jax.shard_map(
        shards,
        mesh=mesh,
        in_specs=(P("narrow", "wide"), P("narrow"), P("narrow"), P(), P(), P()),
        out_specs=P("wide", "narrow"),
        check_vma=False,
    )
```

```python
import jax
import jax.numpy as jnp
from jax import lax
from jax.experimental import pallas as pl
from jax.experimental.pallas import tpu as pltpu
from jax.sharding import PartitionSpec as P

MESH = pl.DeviceIdType.MESH
F32, BF16 = jnp.float32, jnp.bfloat16


def lookup(indices, table_ref, quarter, found):
    size = table_ref.shape[0] // 4

    def body(j, found):
        for k in range(10):
            at = quarter * size + j * 10 + k
            found = jnp.where(indices == at, table_ref[at], found)
        return found
    return lax.fori_loop(0, size // 10, body, found)


def kernel(a_ref, occ_index, vir_index, occ_table, vir_table, omega_ref, out_ref, G, J, W, R, acc, other, land,
           zs, zr, ws, wr, s1s, s1r, s2s, s2r, s3s, s3r, ds, dr, as_, ar, ls, os, levels, relay, br, bs,
           occ_ref, vir_ref, occ_energy, vir_energy, frequency, ts):
    wide, narrow = lax.axis_index("wide"), lax.axis_index("narrow")
    zh, x, y = wide // 16, (wide // 4) % 4, wide % 4
    zl, c = narrow // 2, narrow % 2
    pos = zh * 4 + zl
    h, pi = zl // 2, zl % 2

    def at(x_=x, y_=y, pos_=pos, c_=c):
        return ((pos_ // 4) * 16 + x_ * 4 + y_, (pos_ % 4) * 2 + c_)

    def remote(src, dst, send, recv, device):
        return pltpu.make_async_remote_copy(
            src_ref=src, dst_ref=dst, send_sem=send, recv_sem=recv, device_id=device, device_id_type=MESH)

    xs = [(x + d) % 4 for d in range(4)]
    ys = [(y + d) % 4 for d in range(4)]
    step = jnp.where(zl < 2, 1, 3)
    turn = [(zl + t * step) % 4 for t in range(4)]

    barrier = pltpu.get_barrier_semaphore()
    friends = [at(x_=xs[d]) for d in (1, 2, 3)] + [at(y_=ys[d]) for d in (1, 2, 3)]
    friends += [at(pos_=(pos + d) % 8) for d in range(1, 8)] + [at(c_=1 - c)]
    for device in friends:
        pl.semaphore_signal(barrier, inc=1, device_id=device, device_id_type=MESH)

    def load(hh, r):
        return pltpu.make_async_copy(
            a_ref.at[pl.ds(r * 256, 256), pl.ds(hh * 128, 128)], G.at[pos, hh, r], ls.at[hh, r])

    for hh in range(2):
        for r in range(2):
            load(hh, r).start()
    tables = [pltpu.make_async_copy(src, dst, ts.at[n]) for n, (src, dst) in enumerate((
        (occ_index, occ_ref), (vir_index, vir_ref), (occ_table, occ_energy), (vir_table, vir_energy),
        (omega_ref, frequency)))]
    for table in tables:
        table.start()
    pl.semaphore_wait(barrier, len(friends))
    for hh in range(2):
        for r in range(2):
            load(hh, r).wait()

    CHUNKS = [(d, o, r) for o in range(2) for d in (1, 2, 3) for r in range(2)] + [(4, 0, 0), (4, 0, 1)]

    def z_block(way, d, o, r):
        return G.at[(pos + 8 + (-d if way == 0 else d)) % 8, o if way == 1 else 1 - o, r]

    def z_copy(way, d, o, r):
        block = z_block(way, d, o, r)
        return remote(block, block, zs.at[way, d, o, r], zr.at[way, d, o, r],
                      at(pos_=(pos + (1 if way == 0 else 7)) % 8))

    def z_wait(way, d, o, r):
        block = z_block(way, d, o, r)
        remote(block, block, zs.at[way, d - 1, o, r], zr.at[way, d - 1, o, r], at(pos_=(pos + 1) % 8)).wait_recv()

    def z_sent(d, o):
        return d < 3 or o == 0

    def w_copy(t):
        return remote(W.at[zl], W.at[zl], ws.at[t], wr.at[zl], at(pos_=zh * 4 + (zl + t) % 4))

    def line(r, shift):
        return at(x_=xs[shift]) if r == 0 else at(y_=ys[shift])

    def cross(r, shift):
        return at(y_=ys[shift]) if r == 0 else at(x_=xs[shift])

    def behind(s, r):
        return (x - y - pi - 2 * s + 16) % 4 if r == 0 else (y - x + pi + 2 * s + 4) % 4

    def piece(t, s, r, shift):
        y2 = ys[shift] if r == 0 else (xs[shift] - pi - 2 * s + 8) % 4
        return J.at[turn[t], s, y2, r]

    def first(t, s, r, way):
        p = piece(t, s, r, 0)
        return remote(p, p, s1s.at[t, s, r, way], s1r.at[t, s, r], line(r, 1 if way == 0 else 3))

    def second(t, s, r, way):
        p = piece(t, s, r, 0)
        return remote(p, p, s2s.at[t, s, r, way], s2r.at[t, s, r, way], cross(r, 1 if way == 0 else 3))

    def second_wait(t, s, r, way):
        p = piece(t, s, r, 3 if way == 0 else 1)
        remote(p, p, s2s.at[t, s, r, way], s2r.at[t, s, r, way], cross(r, 1)).wait_recv()

    def third(t, s, r):
        way = (t + r) % 2
        p = piece(t, s, r, 3 if way == 0 else 1)
        return remote(p, p, s3s.at[t, s, r], s3r.at[t, s, r], cross(r, 1 if way == 0 else 3))

    def third_wait(t, s, r):
        p = piece(t, s, r, 2)
        remote(p, p, s3s.at[t, s, r], s3r.at[t, s, r], cross(r, 1)).wait_recv()

    def stage1(t, s, r):
        @pl.when(behind(s, r) == 0)
        def _():
            J[turn[t], s, y, r] = G[zh * 4 + turn[t], h, r]
            for way in range(2):
                first(t, s, r, way).start()

    def stage2(t, s, r):
        @pl.when(behind(s, r) != 0)
        def _():
            p = piece(t, s, r, 0)
            remote(p, p, s1s.at[t, s, r, 0], s1r.at[t, s, r], line(r, 1)).wait_recv()

        way = (t + r) % 2

        @pl.when(behind(s, r) == (1 if way == 0 else 3))
        def _():
            first(t, s, r, way).start()

        for w in range(2):
            second(t, s, r, w).start()

    def stage3(t, s, r):
        second_wait(t, s, r, (t + r) % 2)
        third(t, s, r).start()

    def stage4(t, s, r):
        second_wait(t, s, r, 1 - (t + r) % 2)
        third_wait(t, s, r)

    def prepare(q, hh, r):
        zq, zhq = q % 4, q // 4
        w = jnp.concatenate([W[zq, 2 * r:2 * r + 1], W[zq, 2 * r + 1:2 * r + 2]], axis=1)
        v = G[q, hh, r].T * w
        hi = v.astype(BF16)
        rows = pl.ds(pl.multiple_of(hh * 128, 128), 128)
        R[zq, zhq, 0, rows, r * 256:r * 256 + 256] = hi
        R[zq, zhq, 1, rows, r * 256:r * 256 + 256] = (v - hi.astype(F32)).astype(BF16)

    def unit(t, s, zh1):
        zq = turn[t]

        for p in range(2):
            rows = [jnp.concatenate([J[zq, s, p, r], J[zq, s, p + 2, r]], axis=1) for r in range(2)]
            b = jnp.concatenate(rows, axis=0)
            bh = b.astype(BF16)
            bl = (b - bh.astype(F32)).astype(BF16)
            both = jnp.dot(R[zq, zh1].reshape(512, 512), bh, preferred_element_type=F32)
            acc[s, p, zh1] += both[:256] + both[256:] + jnp.dot(R[zq, zh1, 0], bl, preferred_element_type=F32)

    yc = (pi + c) % 2

    def rows_of(e):
        return 1 - zh if e == 0 else zh

    def d_copy(s, e):
        zh1 = rows_of(e)
        return remote(acc.at[s, 1 - yc, zh1], other.at[s, zh1], ds.at[s, e], dr.at[s, e], at(c_=1 - c))

    def goes_to(s, k, e):
        i = ((2 * k + yc + pi + 2 * s) % 4) // 2
        return rows_of(e) * 4 + 2 * zh + i

    def detour(q):
        return jnp.logical_or(jnp.logical_and(pos == 0, q == 4), jnp.logical_and(pos == 7, q == 3))

    def result(s, k, e):
        return acc.at[s, yc, rows_of(e), :, pl.ds(k * 128, 128)]

    def a_copy(s, k, e):
        return remote(result(s, k, e), land.at[2 * k + yc, h],
                      as_.at[s, k, e], ar.at[zl, k], at(pos_=goes_to(s, k, e)))

    def b_copy(s, k):
        return remote(result(s, k, 0), relay.at[s], as_.at[s, k, 0], br.at[s],
                      at(pos_=jnp.where(pos == 0, 6, 1)))

    def c_copy(s):
        zq, i = jnp.where(pos == 6, 0, 3), jnp.where(pos == 6, 0, 1)
        ycq = (zq % 2 + c) % 2
        k = (i + 2 - ((ycq + zq % 2 + 2 * s) % 4) // 2) % 2
        return remote(relay.at[s], land.at[2 * k + ycq, zq // 2], bs.at[s], ar.at[zq, k],
                      at(pos_=jnp.where(pos == 6, 4, 3)))

    passes = jnp.logical_or(pos == 6, pos == 1)

    def send_out(s, e):
        for k in range(2):
            q = goes_to(s, k, e)

            @pl.when(jnp.logical_and(q != pos, jnp.logical_not(detour(q))))
            def _(k=k):
                a_copy(s, k, e).start()

            if e == 0:
                @pl.when(detour(q))
                def _(k=k):
                    b_copy(s, k).start()
            else:
                @pl.when(q == pos)
                def _(k=k):
                    land[2 * k + yc, h] = acc[s, yc, zh, :, k * 128:k * 128 + 128]

    def pass_on(s):
        @pl.when(passes)
        def _():
            remote(relay.at[s], relay.at[s], bs.at[s], br.at[s], at(c_=1 - c)).wait_recv()
            c_copy(s).start()

    def arrive(n, way):
        d, o, r = CHUNKS[n]
        z_wait(way, d, o, r)
        if d < 3:
            z_copy(way, d, o, r).start()

    def launch(d, o):
        for way in range(2):
            for r in range(2):
                z_copy(way, d, o, r).start()

    def ready(n):
        d, o, r = CHUNKS[n]
        for way in range(2):
            prepare((pos + 8 + (-d if way == 0 else d)) % 8, o if way == 1 else 1 - o, r)

    launch(0, 0)

    def weigh(quarter):
        if quarter == 0:
            levels[...] = jnp.zeros_like(levels)
            for table in tables:
                table.wait()
        levels[0] = lookup(vir_ref[...], vir_energy, quarter, levels[0])
        levels[1] = lookup(occ_ref[...], occ_energy, quarter, levels[1])
        if quarter < 3:
            return
        gap = levels[0] - levels[1]
        omega = frequency[0]
        weights = 2.0 * gap / (gap * gap + omega * omega)
        W[zl] = jnp.concatenate([weights, weights], axis=0)
        for t in range(1, 4):
            w_copy(t).start()

    def begin():
        acc[...] = jnp.zeros_like(acc)
        for t in range(1, 4):
            zq = (zl + t) % 4
            remote(W.at[zq], W.at[zq], ws.at[t], wr.at[zq], at(pos_=zh * 4 + zq)).wait_recv()
        for hh in range(2):
            for r in range(2):
                prepare(pos, hh, r)

    def own(t, s):
        unit(t, s, zh)

    def far(t, s):
        unit(t, s, 1 - zh)

    PLAN = (
        "1001 w0 1000 w1",
        "w2 w3 1010 c",
        "z01 z00 1110 1100",
        "z10 1011 z11 1101",
        "1111 2000 z20 z21",
        "1200 2110 1210 z30",
        "z31 2100 1201 y",
        "2101 2010 3000 z41",
        "2001 1211 p1 z51",
        "2200 z40 z50 p5",
        "z61 z60 1300 1310",
        "p6 2011 z70 z71",
        "1311 p7 1301 2210",
        "3101 2201 p0 2111",
        "p3 3100 z81 z80",
        "2300 z91 2310 3001",
        "z90 p4 p9 p2",
        "p8 x 4000 2301",
        "3201 2311 3200 2211",
        "3011 za1 za0 4100",
        "zb0 3301 3300 zb1",
        "pb 4001 3010 zc0",
        "zd0 zc1 pc pa",
        "zd1 4101 u10 v10",
        "4201 pd v00 4200",
        "v20 4300 4301 v30",
        "d00 u30 3310 u20",
        "o00 3311 u00 d01",
        "3211 3210 3110 3111",
        "4010 o01 4011 4310",
        "v01 4311 v31 4211",
        "4210 v21 r0 4110",
        "4111 v11 d10 u01",
        "u21 u31 o10 u11",
        "d11 o11 r1",
    )
    for token in [word for words in PLAN for word in words.split()]:
        kind, args = token[0], [int(v, 16) for v in token[1:]]
        if kind == "z":
            arrive(*args)
        elif kind == "y":
            launch(0, 1)
        elif kind == "x":
            launch(3, 0)
        elif kind == "w":
            weigh(*args)
        elif kind == "c":
            begin()
        elif kind == "p":
            ready(args[0])
        elif kind in "1234":
            {"1": stage1, "2": stage2, "3": stage3, "4": stage4}[kind](*args)
        elif kind == "u":
            own(*args)
        elif kind == "v":
            far(*args)
        elif kind == "d":
            d_copy(*args).start()
        elif kind == "o":
            s, e = args
            d_copy(s, e).wait_recv()
            acc[s, yc, rows_of(e)] += other[s, rows_of(e)]
            send_out(s, e)
        elif kind == "r":
            pass_on(*args)

    for way in range(2):
        for d in range(4):
            for o in range(2):
                for r in range(2):
                    if z_sent(d, o):
                        z_copy(way, d, o, r).wait_send()
    for t in range(1, 4):
        w_copy(t).wait_send()
    for s in range(2):
        for t in range(4):
            for r in range(2):
                fwd = (t + r) % 2
                for way in range(2):
                    sends = behind(s, r) == 0
                    if way == fwd:
                        sends = jnp.logical_or(sends, behind(s, r) == (1 if way == 0 else 3))

                    @pl.when(sends)
                    def _(t=t, s=s, r=r, way=way):
                        first(t, s, r, way).wait_send()

                    second(t, s, r, way).wait_send()
                third(t, s, r).wait_send()

    def put(zq, k):
        y2, hh = 2 * k + (zq % 2 + c) % 2, zq // 2
        columns = pl.ds(pl.multiple_of(y2 * 256 + hh * 128, 128), 128)
        return pltpu.make_async_copy(land.at[y2, hh], out_ref.at[:, columns], os.at[zq, k])

    def part(zq, s):
        return (((2 * (zl % 2) + c - (zq % 2 + c) % 2 - zq % 2 + 4) % 4) // 2 + s) % 2

    for s in range(2):
        for zq in range(4):
            k = part(zq, s)

            @pl.when((zl // 2) * 4 + zq != pos)
            def _(zq=zq, k=k):
                block = land.at[2 * k + (zq % 2 + c) % 2, zq // 2]
                remote(block, block, as_.at[0, 0, 0], ar.at[zq, k], at(c_=1 - c)).wait_recv()

            put(zq, k).start()
    for zq in range(4):
        for k in range(2):
            put(zq, k).wait()

    for s in range(2):
        for e in range(2):
            d_copy(s, e).wait_send()
            for k in range(2):
                @pl.when(goes_to(s, k, e) != pos)
                def _(s=s, k=k, e=e):
                    a_copy(s, k, e).wait_send()

        @pl.when(passes)
        def _(s=s):
            c_copy(s).wait_send()


def shards(aux_vectors, occ_index, vir_index, occ_energy, vir_energy, frequency):
    dma = pltpu.SemaphoreType.DMA
    hbm = pl.BlockSpec(memory_space=pltpu.HBM)
    return pl.pallas_call(
        kernel,
        out_shape=pltpu.VMEM((256, 1024), F32),
        in_specs=[hbm] * 6,
        out_specs=hbm,
        scratch_shapes=[
            pltpu.VMEM((8, 2, 2, 256, 128), F32),
            pltpu.VMEM((4, 2, 4, 2, 256, 128), F32),
            pltpu.VMEM((4, 8, 128), F32),
            pltpu.VMEM((4, 2, 2, 256, 512), BF16),
            pltpu.VMEM((2, 2, 2, 256, 256), F32),
            pltpu.VMEM((2, 2, 256, 256), F32),
            pltpu.VMEM((4, 2, 256, 128), F32),
            dma((2, 4, 2, 2)), dma((2, 4, 2, 2)),
            dma((4,)), dma((4,)),
            dma((4, 2, 2, 2)), dma((4, 2, 2)),
            dma((4, 2, 2, 2)), dma((4, 2, 2, 2)),
            dma((4, 2, 2)), dma((4, 2, 2)),
            dma((2, 2)), dma((2, 2)),
            dma((2, 2, 2)), dma((4, 2)),
            dma((2, 2)), dma((4, 2)),
            pltpu.VMEM((2, 4, 128), F32),
            pltpu.VMEM((2, 256, 128), F32), dma((2,)), dma((2,)),
            pltpu.VMEM((4, 128), jnp.int32), pltpu.VMEM((4, 128), jnp.int32),
            pltpu.SMEM((200,), F32), pltpu.SMEM((2000,), F32), pltpu.SMEM((1,), F32), dma((5,)),
        ],
        compiler_params=pltpu.CompilerParams(
            collective_id=0, has_side_effects=True, vmem_limit_bytes=62 * 2**20),
        cost_estimate=pl.CostEstimate(flops=2 * 3 * 512 * 1024 * 2048, bytes_accessed=2 * 2**20, transcendentals=0),
        name="gather_multiply",
    )(aux_vectors, occ_index.reshape(4, 128), vir_index.reshape(4, 128), occ_energy, vir_energy, frequency)


def solution(mesh):
    return jax.shard_map(
        shards,
        mesh=mesh,
        in_specs=(P("narrow", "wide"), P("narrow"), P("narrow"), P(), P(), P()),
        out_specs=P("wide", "narrow"),
        check_vma=False,
    )
```

```python
import jax
import jax.numpy as jnp
from jax import lax
from jax.experimental import pallas as pl
from jax.experimental.pallas import tpu as pltpu
from jax.sharding import PartitionSpec as P

MESH = pl.DeviceIdType.MESH
F32, BF16 = jnp.float32, jnp.bfloat16


def lookup(indices, table_ref, quarter, found):
    size = table_ref.shape[0] // 4

    def body(j, found):
        for k in range(10):
            at = quarter * size + j * 10 + k
            found = jnp.where(indices == at, table_ref[at], found)
        return found
    return lax.fori_loop(0, size // 10, body, found)


def kernel(a_ref, occ_index, vir_index, occ_table, vir_table, omega_ref, out_ref, G, J, W, R, acc, other, land,
           zs, zr, ws, wr, s1s, s1r, s2s, s2r, s3s, s3r, ds, dr, as_, ar, ls, os, levels, relay, br, bs,
           occ_ref, vir_ref, occ_energy, vir_energy, frequency, ts):
    wide, narrow = lax.axis_index("wide"), lax.axis_index("narrow")
    zh, x, y = wide // 16, (wide // 4) % 4, wide % 4
    zl, c = narrow // 2, narrow % 2
    pos = zh * 4 + zl
    h, pi = zl // 2, zl % 2

    def at(x_=x, y_=y, pos_=pos, c_=c):
        return ((pos_ // 4) * 16 + x_ * 4 + y_, (pos_ % 4) * 2 + c_)

    def remote(src, dst, send, recv, device):
        return pltpu.make_async_remote_copy(
            src_ref=src, dst_ref=dst, send_sem=send, recv_sem=recv, device_id=device, device_id_type=MESH)

    xs = [(x + d) % 4 for d in range(4)]
    ys = [(y + d) % 4 for d in range(4)]
    step = jnp.where(zl < 2, 1, 3)
    turn = [(zl + t * step) % 4 for t in range(4)]

    barrier = pltpu.get_barrier_semaphore()
    friends = [at(x_=xs[d]) for d in (1, 3)] + [at(y_=ys[d]) for d in (1, 3)]
    friends += [at(pos_=(pos + d) % 8) for d in range(1, 8)] + [at(c_=1 - c)]
    for device in friends:
        pl.semaphore_signal(barrier, inc=1, device_id=device, device_id_type=MESH)

    def load(hh, r):
        return pltpu.make_async_copy(
            a_ref.at[pl.ds(r * 256, 256), pl.ds(hh * 128, 128)], G.at[pos, hh, r], ls.at[hh, r])

    for hh in range(2):
        for r in range(2):
            load(hh, r).start()
    tables = [pltpu.make_async_copy(src, dst, ts.at[n]) for n, (src, dst) in enumerate((
        (occ_index, occ_ref), (vir_index, vir_ref), (occ_table, occ_energy), (vir_table, vir_energy),
        (omega_ref, frequency)))]
    for table in tables:
        table.start()
    pl.semaphore_wait(barrier, len(friends))
    for hh in range(2):
        for r in range(2):
            load(hh, r).wait()

    CHUNKS = [(d, o, r) for o in range(2) for d in (1, 2, 3) for r in range(2)] + [(4, 0, 0), (4, 0, 1)]

    def z_block(way, d, o, r):
        return G.at[(pos + 8 + (-d if way == 0 else d)) % 8, o if way == 1 else 1 - o, r]

    def z_copy(way, d, o, r):
        block = z_block(way, d, o, r)
        return remote(block, block, zs.at[way, d, o, r], zr.at[way, d, o, r],
                      at(pos_=(pos + (1 if way == 0 else 7)) % 8))

    def z_wait(way, d, o, r):
        block = z_block(way, d, o, r)
        remote(block, block, zs.at[way, d - 1, o, r], zr.at[way, d - 1, o, r], at(pos_=(pos + 1) % 8)).wait_recv()

    def z_sent(d, o):
        return d < 3 or o == 0

    def w_copy(t):
        return remote(W.at[zl], W.at[zl], ws.at[t], wr.at[zl], at(pos_=zh * 4 + (zl + t) % 4))

    def line(r, shift):
        return at(x_=xs[shift]) if r == 0 else at(y_=ys[shift])

    def cross(r, shift):
        return at(y_=ys[shift]) if r == 0 else at(x_=xs[shift])

    def behind(s, r):
        return (x - y - pi - 2 * s + 16) % 4 if r == 0 else (y - x + pi + 2 * s + 4) % 4

    def piece(t, s, r, shift):
        y2 = ys[shift] if r == 0 else (xs[shift] - pi - 2 * s + 8) % 4
        return J.at[turn[t], s, y2, r]

    def first(t, s, r, way):
        p = piece(t, s, r, 0)
        return remote(p, p, s1s.at[t, s, r, way], s1r.at[t, s, r], line(r, 1 if way == 0 else 3))

    def second(t, s, r, way):
        p = piece(t, s, r, 0)
        return remote(p, p, s2s.at[t, s, r, way], s2r.at[t, s, r, way], cross(r, 1 if way == 0 else 3))

    def second_wait(t, s, r, way):
        p = piece(t, s, r, 3 if way == 0 else 1)
        remote(p, p, s2s.at[t, s, r, way], s2r.at[t, s, r, way], cross(r, 1)).wait_recv()

    def third(t, s, r):
        way = (t + r) % 2
        p = piece(t, s, r, 3 if way == 0 else 1)
        return remote(p, p, s3s.at[t, s, r], s3r.at[t, s, r], cross(r, 1 if way == 0 else 3))

    def third_wait(t, s, r):
        p = piece(t, s, r, 2)
        remote(p, p, s3s.at[t, s, r], s3r.at[t, s, r], cross(r, 1)).wait_recv()

    def stage1(t, s, r):
        @pl.when(behind(s, r) == 0)
        def _():
            J[turn[t], s, y, r] = G[zh * 4 + turn[t], h, r]
            for way in range(2):
                first(t, s, r, way).start()

    def stage2(t, s, r):
        @pl.when(behind(s, r) != 0)
        def _():
            p = piece(t, s, r, 0)
            remote(p, p, s1s.at[t, s, r, 0], s1r.at[t, s, r], line(r, 1)).wait_recv()

        way = (t + r) % 2

        @pl.when(behind(s, r) == (1 if way == 0 else 3))
        def _():
            first(t, s, r, way).start()

        for w in range(2):
            second(t, s, r, w).start()

    def stage3(t, s, r):
        second_wait(t, s, r, (t + r) % 2)
        third(t, s, r).start()

    def stage4(t, s, r):
        second_wait(t, s, r, 1 - (t + r) % 2)
        third_wait(t, s, r)

    def prepare(q, hh, r):
        zq, zhq = q % 4, q // 4
        w = jnp.concatenate([W[zq, 2 * r:2 * r + 1], W[zq, 2 * r + 1:2 * r + 2]], axis=1)
        v = G[q, hh, r].T * w
        hi = v.astype(BF16)
        rows = pl.ds(pl.multiple_of(hh * 128, 128), 128)
        R[zq, zhq, 0, rows, r * 256:r * 256 + 256] = hi
        R[zq, zhq, 1, rows, r * 256:r * 256 + 256] = (v - hi.astype(F32)).astype(BF16)

    def unit(t, s, zh1):
        zq = turn[t]

        for p in range(2):
            rows = [jnp.concatenate([J[zq, s, p, r], J[zq, s, p + 2, r]], axis=1) for r in range(2)]
            b = jnp.concatenate(rows, axis=0)
            bh = b.astype(BF16)
            bl = (b - bh.astype(F32)).astype(BF16)
            both = jnp.dot(R[zq, zh1].reshape(512, 512), bh, preferred_element_type=F32)
            acc[s, p, zh1] += both[:256] + both[256:] + jnp.dot(R[zq, zh1, 0], bl, preferred_element_type=F32)

    yc = (pi + c) % 2

    def rows_of(e):
        return 1 - zh if e == 0 else zh

    def d_copy(s, e):
        zh1 = rows_of(e)
        return remote(acc.at[s, 1 - yc, zh1], other.at[s, zh1], ds.at[s, e], dr.at[s, e], at(c_=1 - c))

    def goes_to(s, k, e):
        i = ((2 * k + yc + pi + 2 * s) % 4) // 2
        return rows_of(e) * 4 + 2 * zh + i

    def detour(q):
        return jnp.logical_or(jnp.logical_and(pos == 0, q == 4), jnp.logical_and(pos == 7, q == 3))

    def result(s, k, e):
        return acc.at[s, yc, rows_of(e), :, pl.ds(k * 128, 128)]

    def a_copy(s, k, e):
        return remote(result(s, k, e), land.at[2 * k + yc, h],
                      as_.at[s, k, e], ar.at[zl, k], at(pos_=goes_to(s, k, e)))

    def b_copy(s, k):
        return remote(result(s, k, 0), relay.at[s], as_.at[s, k, 0], br.at[s],
                      at(pos_=jnp.where(pos == 0, 6, 1)))

    def c_copy(s):
        zq, i = jnp.where(pos == 6, 0, 3), jnp.where(pos == 6, 0, 1)
        ycq = (zq % 2 + c) % 2
        k = (i + 2 - ((ycq + zq % 2 + 2 * s) % 4) // 2) % 2
        return remote(relay.at[s], land.at[2 * k + ycq, zq // 2], bs.at[s], ar.at[zq, k],
                      at(pos_=jnp.where(pos == 6, 4, 3)))

    passes = jnp.logical_or(pos == 6, pos == 1)

    def send_out(s, e):
        for k in range(2):
            q = goes_to(s, k, e)

            @pl.when(jnp.logical_and(q != pos, jnp.logical_not(detour(q))))
            def _(k=k):
                a_copy(s, k, e).start()

            if e == 0:
                @pl.when(detour(q))
                def _(k=k):
                    b_copy(s, k).start()
            else:
                @pl.when(q == pos)
                def _(k=k):
                    land[2 * k + yc, h] = acc[s, yc, zh, :, k * 128:k * 128 + 128]

    def pass_on(s):
        @pl.when(passes)
        def _():
            remote(relay.at[s], relay.at[s], bs.at[s], br.at[s], at(c_=1 - c)).wait_recv()
            c_copy(s).start()

    def arrive(n, way):
        d, o, r = CHUNKS[n]
        z_wait(way, d, o, r)
        if d < 3:
            z_copy(way, d, o, r).start()

    def launch(d, o):
        for way in range(2):
            for r in range(2):
                z_copy(way, d, o, r).start()

    def ready(n):
        d, o, r = CHUNKS[n]
        for way in range(2):
            prepare((pos + 8 + (-d if way == 0 else d)) % 8, o if way == 1 else 1 - o, r)

    launch(0, 0)

    def weigh(quarter):
        if quarter == 0:
            levels[...] = jnp.zeros_like(levels)
            for table in tables:
                table.wait()
        levels[0] = lookup(vir_ref[...], vir_energy, quarter, levels[0])
        levels[1] = lookup(occ_ref[...], occ_energy, quarter, levels[1])
        if quarter < 3:
            return
        gap = levels[0] - levels[1]
        omega = frequency[0]
        weights = 2.0 * gap / (gap * gap + omega * omega)
        W[zl] = jnp.concatenate([weights, weights], axis=0)
        for t in range(1, 4):
            w_copy(t).start()

    def begin():
        acc[...] = jnp.zeros_like(acc)
        for t in range(1, 4):
            zq = (zl + t) % 4
            remote(W.at[zq], W.at[zq], ws.at[t], wr.at[zq], at(pos_=zh * 4 + zq)).wait_recv()
        for hh in range(2):
            for r in range(2):
                prepare(pos, hh, r)

    def own(t, s):
        unit(t, s, zh)

    def far(t, s):
        unit(t, s, 1 - zh)

    PLAN = (
        "1001 w0 1000 w1",
        "w2 w3 1010 c",
        "z01 z00 1110 1100",
        "z10 1011 z11 1101",
        "1111 2000 z20 z21",
        "1200 2110 1210 z30",
        "z31 2100 1201 y",
        "2101 2010 3000 z41",
        "2001 1211 p1 z51",
        "2200 z40 z50 p5",
        "z61 z60 1300 1310",
        "p6 2011 z70 z71",
        "1311 p7 1301 2210",
        "3101 2201 p0 2111",
        "p3 3100 z81 z80",
        "2300 z91 2310 3001",
        "z90 p4 p9 p2",
        "p8 x 4000 2301",
        "3201 2311 3200 2211",
        "3011 za1 za0 4100",
        "zb0 3301 3300 zb1",
        "pb 4001 3010 zc0",
        "zd0 zc1 pc pa",
        "zd1 4101 u10 v10",
        "4201 pd v00 4200",
        "v20 4300 4301 v30",
        "d00 u30 u20 o00",
        "3310 3311 u00 d01",
        "3211 3210 3110 3111",
        "4010 o01 4011 4310",
        "v01 4311 v31 4211",
        "4210 v21 r0 4110",
        "4111 v11 d10 u01",
        "u21 u31 o10 u11",
        "d11 o11 r1",
    )
    for token in [word for words in PLAN for word in words.split()]:
        kind, args = token[0], [int(v, 16) for v in token[1:]]
        if kind == "z":
            arrive(*args)
        elif kind == "y":
            launch(0, 1)
        elif kind == "x":
            launch(3, 0)
        elif kind == "w":
            weigh(*args)
        elif kind == "c":
            begin()
        elif kind == "p":
            ready(args[0])
        elif kind in "1234":
            {"1": stage1, "2": stage2, "3": stage3, "4": stage4}[kind](*args)
        elif kind == "u":
            own(*args)
        elif kind == "v":
            far(*args)
        elif kind == "d":
            d_copy(*args).start()
        elif kind == "o":
            s, e = args
            d_copy(s, e).wait_recv()
            acc[s, yc, rows_of(e)] += other[s, rows_of(e)]
            send_out(s, e)
        elif kind == "r":
            pass_on(*args)

    for way in range(2):
        for d in range(4):
            for o in range(2):
                for r in range(2):
                    if z_sent(d, o):
                        z_copy(way, d, o, r).wait_send()
    for t in range(1, 4):
        w_copy(t).wait_send()
    for s in range(2):
        for t in range(4):
            for r in range(2):
                fwd = (t + r) % 2
                for way in range(2):
                    sends = behind(s, r) == 0
                    if way == fwd:
                        sends = jnp.logical_or(sends, behind(s, r) == (1 if way == 0 else 3))

                    @pl.when(sends)
                    def _(t=t, s=s, r=r, way=way):
                        first(t, s, r, way).wait_send()

                    second(t, s, r, way).wait_send()
                third(t, s, r).wait_send()

    def put(zq, k):
        y2, hh = 2 * k + (zq % 2 + c) % 2, zq // 2
        columns = pl.ds(pl.multiple_of(y2 * 256 + hh * 128, 128), 128)
        return pltpu.make_async_copy(land.at[y2, hh], out_ref.at[:, columns], os.at[zq, k])

    def part(zq, s):
        return (((2 * (zl % 2) + c - (zq % 2 + c) % 2 - zq % 2 + 4) % 4) // 2 + s) % 2

    for s in range(2):
        for zq in range(4):
            k = part(zq, s)

            @pl.when((zl // 2) * 4 + zq != pos)
            def _(zq=zq, k=k):
                block = land.at[2 * k + (zq % 2 + c) % 2, zq // 2]
                remote(block, block, as_.at[0, 0, 0], ar.at[zq, k], at(c_=1 - c)).wait_recv()

            put(zq, k).start()
    for zq in range(4):
        for k in range(2):
            put(zq, k).wait()

    for s in range(2):
        for e in range(2):
            d_copy(s, e).wait_send()
            for k in range(2):
                @pl.when(goes_to(s, k, e) != pos)
                def _(s=s, k=k, e=e):
                    a_copy(s, k, e).wait_send()

        @pl.when(passes)
        def _(s=s):
            c_copy(s).wait_send()


def shards(aux_vectors, occ_index, vir_index, occ_energy, vir_energy, frequency):
    dma = pltpu.SemaphoreType.DMA
    hbm = pl.BlockSpec(memory_space=pltpu.HBM)
    return pl.pallas_call(
        kernel,
        out_shape=pltpu.VMEM((256, 1024), F32),
        in_specs=[hbm] * 6,
        out_specs=hbm,
        scratch_shapes=[
            pltpu.VMEM((8, 2, 2, 256, 128), F32),
            pltpu.VMEM((4, 2, 4, 2, 256, 128), F32),
            pltpu.VMEM((4, 8, 128), F32),
            pltpu.VMEM((4, 2, 2, 256, 512), BF16),
            pltpu.VMEM((2, 2, 2, 256, 256), F32),
            pltpu.VMEM((2, 2, 256, 256), F32),
            pltpu.VMEM((4, 2, 256, 128), F32),
            dma((2, 4, 2, 2)), dma((2, 4, 2, 2)),
            dma((4,)), dma((4,)),
            dma((4, 2, 2, 2)), dma((4, 2, 2)),
            dma((4, 2, 2, 2)), dma((4, 2, 2, 2)),
            dma((4, 2, 2)), dma((4, 2, 2)),
            dma((2, 2)), dma((2, 2)),
            dma((2, 2, 2)), dma((4, 2)),
            dma((2, 2)), dma((4, 2)),
            pltpu.VMEM((2, 4, 128), F32),
            pltpu.VMEM((2, 256, 128), F32), dma((2,)), dma((2,)),
            pltpu.VMEM((4, 128), jnp.int32), pltpu.VMEM((4, 128), jnp.int32),
            pltpu.SMEM((200,), F32), pltpu.SMEM((2000,), F32), pltpu.SMEM((1,), F32), dma((5,)),
        ],
        compiler_params=pltpu.CompilerParams(
            collective_id=0, has_side_effects=True, vmem_limit_bytes=62 * 2**20),
        cost_estimate=pl.CostEstimate(flops=2 * 3 * 512 * 1024 * 2048, bytes_accessed=2 * 2**20, transcendentals=0),
        name="gather_multiply",
    )(aux_vectors, occ_index.reshape(4, 128), vir_index.reshape(4, 128), occ_energy, vir_energy, frequency)


def solution(mesh):
    return jax.shard_map(
        shards,
        mesh=mesh,
        in_specs=(P("narrow", "wide"), P("narrow"), P("narrow"), P(), P(), P()),
        out_specs=P("wide", "narrow"),
        check_vma=False,
    )
```
